32 devices in a mesh: slot: 4 (over y, x), row: 8 (over z, core).
Axes of the slice: x: 2, y: 2, z: 4, core: 2. Of those that a mesh axis runs over, the one named last changes fastest.
Arguments:
- innovation: bfloat16 [4, 3, 1408, 1408], P('slot', None, 'row'), may hold values from -6 to 6
- clear_mask: int32 [4, 3, 1408, 1408], P('slot', None, 'row'), may hold values 0 or 1
- lag_list: int32 [4], replicated, may hold values from 0 to 3, as said below
Outputs:
- cross_spectra: float32 [2, 4, 3, 1408, 1408], P(None, None, None, 'slot', 'row')
The draws below stay inside these ranges and needn't reach their ends.
Inputs may be any that keep to these rules, and one draw needn't show every extreme that they name: `lag_list`: both 0 and 3 appear in every list; entries may repeat.
All inputs are finite; a program needn't handle non-finite values. No bound on the sum of `clear_mask` on one device may be relied on, other than what follows from the above.
Results may differ from the reference program's by a relative error of at most 0.009.
Values may be sent and summed in bfloat16 or wider, within the bound.
A program may use at most 512 MiB of HBM per device.

```python
import math
import jax
import jax.numpy as jnp
from jax import lax

R = 1408
C = 1408
CH = 3
LAGS = 4
SLOTS = 4


def draw_lag_list(key, part):
    key = jax.random.fold_in(key, 7)
    first_key, second_key, third_key = jax.random.split(key, 3)
    values = jax.random.randint(first_key, (LAGS,), 0, SLOTS)
    top_at = jax.random.randint(second_key, (), 0, LAGS)
    zero_at = (top_at + 1 + jax.random.randint(third_key, (), 0, LAGS - 1)) % LAGS
    positions = jnp.arange(LAGS)
    values = jnp.where(positions == top_at, SLOTS - 1, values)
    values = jnp.where(positions == zero_at, 0, values)
    return values.astype(jnp.int32)


def plant(array, own_key, low, top_value):
    longest = array.shape.index(max(array.shape))
    spots = []
    for shift in (0, 1):
        where = [jax.random.randint(jax.random.fold_in(own_key, axis), (), 0, length) for axis, length in enumerate(array.shape)]
        where[longest] = (where[longest] + shift) % array.shape[longest]
        spots.append(tuple(where))
    return array.at[spots[0]].set(low).at[spots[1]].set(top_value)


def shard_levels(key, extent, shards, least, largest):
    def one(axis_at, parts):
        draws = jax.random.uniform(jax.random.fold_in(jax.random.fold_in(key, 6), axis_at), (parts,), jnp.float32, least / len(shards), largest / len(shards))
        return jnp.repeat(jnp.exp(draws), extent[axis_at] // parts).reshape((-1,) + (1,) * (len(extent) - axis_at - 1))

    loudness = one(*shards[0])
    for cut in shards[1:]:
        loudness = loudness * one(*cut)
    return loudness


def centred(key, shape, deviation, reach, cuts=(), kind=jnp.bfloat16):
    entries = jax.random.normal(key, shape, jnp.float32) * deviation
    if len(cuts) > 0:
        entries = shard_levels(key, shape, cuts, -0.22, 0.18) * entries
    return jnp.clip(entries, min=-reach, max=reach).astype(kind)


def setup_inputs(seed: int = 0) -> dict:
    arg_keys = jax.random.split(jax.random.key(seed), 4)
    innovation = centred(arg_keys[0], (SLOTS, CH, R, C), 1.0, 6.0, ((0, 4), (2, 8)))
    clear_mask = plant((jax.random.randint(arg_keys[1], (SLOTS, CH, R, C), 0, 4) < 3).astype(jnp.int32), jax.random.fold_in(arg_keys[1], 1), 0, 1)
    lag_list = draw_lag_list(jax.random.fold_in(arg_keys[3], 71), 0)
    return dict(innovation=innovation, clear_mask=clear_mask, lag_list=lag_list)


def tables(length):
    indices = jnp.arange(length, dtype=jnp.int32)
    phases = indices[:, None] * indices[None, :] % length
    angles = phases.astype(jnp.float32) * (2.0 * math.pi / length)
    norm_scale = 1.0 / math.sqrt(length)
    return ((jnp.cos(angles) * norm_scale).astype(jnp.bfloat16), (jnp.sin(angles) * norm_scale).astype(jnp.bfloat16))

def spectrum(masked, cosine_cols, sine_cols, cosine_rows, sine_rows):
    flattened = masked.reshape(-1, C)
    g_real = jnp.dot(flattened, cosine_cols, preferred_element_type=jnp.float32).astype(jnp.bfloat16).reshape(CH, R, C)
    g_imag = (-jnp.dot(flattened, sine_cols, preferred_element_type=jnp.float32)).astype(jnp.bfloat16).reshape(CH, R, C)
    cos_wide = cosine_rows.astype(jnp.float32)
    sin_wide = sine_rows.astype(jnp.float32)
    real_wide = g_real.astype(jnp.float32)
    imag_wide = g_imag.astype(jnp.float32)
    f_real = jnp.einsum('kr,crq->ckq', cos_wide, real_wide) + jnp.einsum('kr,crq->ckq', sin_wide, imag_wide)
    f_imag = jnp.einsum('kr,crq->ckq', cos_wide, imag_wide) - jnp.einsum('kr,crq->ckq', sin_wide, real_wide)
    return jnp.stack([f_real, f_imag]).astype(jnp.bfloat16)

def reference(innovation, clear_mask, lag_list):
    masked = innovation * clear_mask.astype(jnp.bfloat16)
    cosine_cols, sine_cols = tables(C)
    cosine_rows, sine_rows = tables(R)
    spectra = lax.map(lambda slab: spectrum(slab, cosine_cols, sine_cols, cosine_rows, sine_rows), masked)

    def lag_sum(lag_value):
        lag_value = lag_value.astype(jnp.int32)

        def accumulate(slot_index, running):
            slot_index = jnp.asarray(slot_index).astype(jnp.int32)
            later_index = jnp.minimum(slot_index + lag_value, SLOTS - 1).astype(jnp.int32)
            earlier = lax.dynamic_index_in_dim(spectra, slot_index, 0, keepdims=False).astype(jnp.float32)
            later = lax.dynamic_index_in_dim(spectra, later_index, 0, keepdims=False).astype(jnp.float32)
            pair_real = earlier[0] * later[0] + earlier[1] * later[1]
            pair_imag = earlier[1] * later[0] - earlier[0] * later[1]
            rounded = lax.optimization_barrier(jnp.stack([pair_real, pair_imag]).astype(jnp.bfloat16)).astype(jnp.float32)
            inside = slot_index + lag_value < SLOTS
            return running + jnp.where(inside, rounded, jnp.zeros_like(rounded))
        summed = lax.fori_loop(0, SLOTS, accumulate, jnp.zeros((2, CH, R, C), jnp.float32))
        return summed / (SLOTS - lag_value).astype(jnp.float32)
    results = lax.map(lag_sum, lag_list)
    return jnp.transpose(results, (1, 0, 2, 3, 4))
```

```python
import math

import jax
import jax.numpy as jnp
import ml_dtypes
import numpy as np
from jax import lax
from jax.sharding import PartitionSpec as P


def tables(length):
    indices = np.arange(length, dtype=np.int64)
    phases = indices[:, None] * indices[None, :] % length
    angles = phases.astype(np.float32) * np.float32(2.0 * math.pi / length)
    norm_scale = np.float32(1.0 / math.sqrt(length))
    return np.cos(angles) * norm_scale, np.sin(angles) * norm_scale


def column_table(length, parts):
    cosine, sine = tables(length)
    both = np.stack([cosine, -sine]).reshape(2, length, parts, length // parts)
    both = both.transpose(2, 0, 1, 3).reshape(parts * 2, length, length // parts)
    return np.ascontiguousarray(both).astype(ml_dtypes.bfloat16)


def row_table(length, parts, slots):
    cosine, sine = tables(length)
    both = np.stack([np.stack([cosine, sine]), np.stack([-sine, cosine])])
    both = both.reshape(2, 2, slots, length // slots, parts, length // parts)
    both = both.transpose(2, 0, 3, 4, 1, 5).reshape(2 * slots, length // slots, 2 * length)
    return np.ascontiguousarray(both).astype(ml_dtypes.bfloat16)


def on_device(innovation, clear_mask, lag_list):
    masked = innovation[0] * clear_mask[0].astype(jnp.bfloat16)
    channels, rows_here, col_count = masked.shape
    row_parts = lax.axis_size("row")
    slot_count = lax.axis_size("slot")
    rows = rows_here * row_parts
    cols_here = col_count // row_parts
    to_columns = jnp.asarray(column_table(col_count, row_parts))
    to_rows = jnp.asarray(row_table(rows, row_parts, slot_count))
    distances = []
    for channel in range(channels):
        spread = jnp.broadcast_to(masked[channel], (2 * row_parts, rows_here, col_count))
        g = lax.dot_general(
            spread,
            to_columns,
            (((2,), (1,)), ((0,), (0,))),
            preferred_element_type=jnp.float32,
        ).astype(jnp.bfloat16)
        g = g.reshape(row_parts, 2, rows_here, cols_here)
        g = lax.all_to_all(g, "row", split_axis=0, concat_axis=0, tiled=True)
        g = jnp.broadcast_to(
            g.reshape(2 * rows, cols_here), (2 * slot_count, 2 * rows, cols_here)
        )
        f = lax.dot_general(
            to_rows,
            g,
            (((2,), (1,)), ((0,), (0,))),
            preferred_element_type=jnp.float32,
        ).astype(jnp.bfloat16)
        f = f.reshape(slot_count, 2, rows // slot_count, cols_here)
        f = lax.all_to_all(f, "slot", split_axis=0, concat_axis=0, tiled=True)
        wide = f.astype(jnp.float32)
        sums = []
        for distance in range(slot_count):
            real = imag = 0.0
            for at in range(slot_count - distance):
                early, late = wide[at], wide[at + distance]
                pair_real = early[0] * late[0] + early[1] * late[1]
                pair_imag = early[1] * late[0] - early[0] * late[1]
                real = real + pair_real.astype(jnp.bfloat16).astype(jnp.float32)
                imag = imag + pair_imag.astype(jnp.bfloat16).astype(jnp.float32)
            weight = 1.0 / (slot_count - distance)
            sums.append((real * weight, imag * weight))
        distances.append(lax.optimization_barrier(sums))
    parts = []
    for part in range(2):
        entries = []
        for entry in range(lag_list.shape[0]):
            for channel in range(channels):
                chosen = distances[channel][0][part]
                for distance in range(1, slot_count):
                    chosen = jnp.where(
                        lag_list[entry] == distance, distances[channel][distance][part], chosen
                    )
                entries.append(chosen)
        parts.extend(entries)
    return jnp.stack(parts).reshape(2, lag_list.shape[0], channels, rows // slot_count, cols_here)


def solution(mesh):
    placed = (P("slot", None, "row", None), P("slot", None, "row", None), P())
    return jax.shard_map(
        on_device,
        mesh=mesh,
        in_specs=placed,
        out_specs=P(None, None, None, "slot", "row"),
        check_vma=False,
    )
```

```python
import math

import jax
import jax.numpy as jnp
import ml_dtypes
import numpy as np
from jax import lax
from jax.sharding import PartitionSpec as P


def tables(length):
    indices = np.arange(length, dtype=np.int64)
    phases = indices[:, None] * indices[None, :] % length
    angles = phases.astype(np.float32) * np.float32(2.0 * math.pi / length)
    norm_scale = np.float32(1.0 / math.sqrt(length))
    return np.cos(angles) * norm_scale, np.sin(angles) * norm_scale


def column_table(length, parts):
    cosine, sine = tables(length)
    both = np.stack([cosine, -sine]).reshape(2, length, parts, length // parts)
    both = both.transpose(2, 1, 0, 3).reshape(parts, length, 2 * (length // parts))
    return np.ascontiguousarray(both).astype(ml_dtypes.bfloat16)


def row_table(length, parts, slots):
    cosine, sine = tables(length)
    both = np.stack([np.stack([cosine, sine]), np.stack([-sine, cosine])])
    both = both.reshape(2, 2, slots, length // slots, length)
    both = both.transpose(2, 0, 3, 1, 4).reshape(2 * slots, length // slots, 2 * length)
    return np.ascontiguousarray(both).astype(ml_dtypes.bfloat16)


def to_slot_owners(spectrum, count):
    here = lax.axis_index("slot")
    blocks = spectrum
    for step in range(1, count):
        if count & (count - 1) == 0:
            pairs = [(at, at ^ step) for at in range(count)]
            target = source = here ^ step
        else:
            pairs = [(at, (at + step) % count) for at in range(count)]
            target, source = (here + step) % count, (here - step) % count
        block = lax.dynamic_index_in_dim(spectrum, target, 0, keepdims=True)
        arrived = lax.ppermute(block, "slot", pairs)
        blocks = lax.dynamic_update_slice_in_dim(blocks, arrived, source, 0)
    return blocks


def on_device(innovation, clear_mask, lag_list):
    masked = innovation[0] * clear_mask[0].astype(jnp.bfloat16)
    channels, rows_here, col_count = masked.shape
    row_parts = lax.axis_size("row")
    slot_count = lax.axis_size("slot")
    rows = rows_here * row_parts
    cols_here = col_count // row_parts
    to_columns = jnp.asarray(column_table(col_count, row_parts))
    to_rows = jnp.asarray(row_table(rows, row_parts, slot_count))
    columns = []
    for channel in range(channels):
        spread = jnp.broadcast_to(masked[channel], (row_parts, rows_here, col_count))
        columns.append(
            lax.dot_general(
                spread,
                to_columns,
                (((2,), (1,)), ((0,), (0,))),
                preferred_element_type=jnp.float32,
            ).astype(jnp.bfloat16)
        )
    spectra = []
    for channel in range(channels):
        g = columns[channel]
        if channel >= 2:
            g, spectra[channel - 2] = lax.optimization_barrier((g, spectra[channel - 2]))
        g = lax.all_to_all(g, "row", split_axis=0, concat_axis=0, tiled=True)
        g = g.reshape(rows, 2 * cols_here)
        g = jnp.concatenate([g[:, :cols_here], g[:, cols_here:]], axis=0)
        g = jnp.broadcast_to(g, (2 * slot_count, 2 * rows, cols_here))
        f = lax.dot_general(
            to_rows,
            g,
            (((2,), (1,)), ((0,), (0,))),
            preferred_element_type=jnp.float32,
        ).astype(jnp.bfloat16)
        spectra.append(f.reshape(slot_count, 2, rows // slot_count, cols_here))
    distances = []
    for channel in range(channels):
        f = to_slot_owners(spectra[channel], slot_count)
        wide = f.astype(jnp.float32)
        sums = []
        for distance in range(slot_count):
            real = imag = 0.0
            for at in range(slot_count - distance):
                early, late = wide[at], wide[at + distance]
                pair_real = early[0] * late[0] + early[1] * late[1]
                pair_imag = early[1] * late[0] - early[0] * late[1]
                real = real + pair_real.astype(jnp.bfloat16).astype(jnp.float32)
                imag = imag + pair_imag.astype(jnp.bfloat16).astype(jnp.float32)
            weight = 1.0 / (slot_count - distance)
            sums.append((real * weight, imag * weight))
        distances.append(lax.optimization_barrier(sums))
    parts = []
    for part in range(2):
        entries = []
        for entry in range(lag_list.shape[0]):
            for channel in range(channels):
                chosen = distances[channel][0][part]
                for distance in range(1, slot_count):
                    chosen = jnp.where(
                        lag_list[entry] == distance, distances[channel][distance][part], chosen
                    )
                entries.append(chosen)
        parts.extend(entries)
    return jnp.stack(parts).reshape(2, lag_list.shape[0], channels, rows // slot_count, cols_here)


def solution(mesh):
    placed = (P("slot", None, "row", None), P("slot", None, "row", None), P())
    return jax.shard_map(
        on_device,
        mesh=mesh,
        in_specs=placed,
        out_specs=P(None, None, None, "slot", "row"),
        check_vma=False,
    )
```

```python
import math

import jax
import jax.numpy as jnp
import ml_dtypes
import numpy as np
from jax import lax
from jax.sharding import PartitionSpec as P


def tables(length):
    indices = np.arange(length, dtype=np.int64)
    phases = indices[:, None] * indices[None, :] % length
    angles = phases.astype(np.float32) * np.float32(2.0 * math.pi / length)
    norm_scale = np.float32(1.0 / math.sqrt(length))
    return np.cos(angles) * norm_scale, np.sin(angles) * norm_scale


def column_table(length, parts):
    cosine, sine = tables(length)
    both = np.stack([cosine, -sine]).reshape(2, length, parts, length // parts)
    both = both.transpose(2, 1, 0, 3).reshape(parts, length, 2 * (length // parts))
    return np.ascontiguousarray(both).astype(ml_dtypes.bfloat16)


def row_table(length, parts, slots):
    cosine, sine = tables(length)
    both = np.stack([np.stack([cosine, sine]), np.stack([-sine, cosine])])
    both = both.reshape(2, 2, slots, length // slots, length)
    both = both.transpose(2, 0, 3, 1, 4).reshape(2 * slots, length // slots, 2 * length)
    return np.ascontiguousarray(both).astype(ml_dtypes.bfloat16)


def to_slot_owners(spectrum, count):
    here = lax.axis_index("slot")
    blocks = spectrum
    for step in range(1, count):
        if count & (count - 1) == 0:
            pairs = [(at, at ^ step) for at in range(count)]
            target = source = here ^ step
        else:
            pairs = [(at, (at + step) % count) for at in range(count)]
            target, source = (here + step) % count, (here - step) % count
        block = lax.dynamic_index_in_dim(spectrum, target, 0, keepdims=True)
        arrived = lax.ppermute(block, "slot", pairs)
        blocks = lax.dynamic_update_slice_in_dim(blocks, arrived, source, 0)
    return blocks


def on_device(innovation, clear_mask, lag_list):
    masked = innovation[0] * clear_mask[0].astype(jnp.bfloat16)
    channels, rows_here, col_count = masked.shape
    row_parts = lax.axis_size("row")
    slot_count = lax.axis_size("slot")
    rows = rows_here * row_parts
    cols_here = col_count // row_parts
    to_columns = jnp.asarray(column_table(col_count, row_parts))
    to_rows = jnp.asarray(row_table(rows, row_parts, slot_count))
    columns = []
    for channel in range(channels):
        spread = jnp.broadcast_to(masked[channel], (row_parts, rows_here, col_count))
        columns.append(
            lax.dot_general(
                spread,
                to_columns,
                (((2,), (1,)), ((0,), (0,))),
                preferred_element_type=jnp.float32,
            ).astype(jnp.bfloat16)
        )
    spectra = []
    for channel in range(channels):
        g = columns[channel]
        g = lax.all_to_all(g, "row", split_axis=0, concat_axis=0, tiled=True)
        g = g.reshape(rows, 2 * cols_here)
        g = jnp.concatenate([g[:, :cols_here], g[:, cols_here:]], axis=0)
        g = jnp.broadcast_to(g, (2 * slot_count, 2 * rows, cols_here))
        f = lax.dot_general(
            to_rows,
            g,
            (((2,), (1,)), ((0,), (0,))),
            preferred_element_type=jnp.float32,
        ).astype(jnp.bfloat16)
        spectra.append(f.reshape(slot_count, 2, rows // slot_count, cols_here))
    distances = []
    for channel in range(channels):
        f = to_slot_owners(spectra[channel], slot_count)
        wide = f.astype(jnp.float32)
        sums = []
        for distance in range(slot_count):
            real = imag = 0.0
            for at in range(slot_count - distance):
                early, late = wide[at], wide[at + distance]
                pair_real = early[0] * late[0] + early[1] * late[1]
                pair_imag = early[1] * late[0] - early[0] * late[1]
                real = real + pair_real.astype(jnp.bfloat16).astype(jnp.float32)
                imag = imag + pair_imag.astype(jnp.bfloat16).astype(jnp.float32)
            weight = 1.0 / (slot_count - distance)
            sums.append((real * weight, imag * weight))
        distances.append(lax.optimization_barrier(sums))
    parts = []
    for part in range(2):
        entries = []
        for entry in range(lag_list.shape[0]):
            for channel in range(channels):
                chosen = distances[channel][0][part]
                for distance in range(1, slot_count):
                    chosen = jnp.where(
                        lag_list[entry] == distance, distances[channel][distance][part], chosen
                    )
                entries.append(chosen)
        parts.extend(entries)
    return jnp.stack(parts).reshape(2, lag_list.shape[0], channels, rows // slot_count, cols_here)


def solution(mesh):
    placed = (P("slot", None, "row", None), P("slot", None, "row", None), P())
    return jax.shard_map(
        on_device,
        mesh=mesh,
        in_specs=placed,
        out_specs=P(None, None, None, "slot", "row"),
        check_vma=False,
    )
```
